512 devices in a mesh: ep: 128 (over z, y, core), dp: 4 (over x).
Axes of the slice: x: 4, y: 8, z: 8, core: 2. Of those that a mesh axis runs over, the one named last changes fastest.
Arguments:
- tokens: bfloat16 [65536, 2048], P(('dp', 'ep')), parts along dimension 0, may hold values from -6 to 6
- expert_ids: int32 [65536, 4], P(('dp', 'ep')), parts along dimension 0, may hold values from 0 to 127, all different within a row; in each aligned block of 128 rows (0 to 127, 128 to 255, ...) at most 6 rows name the same one
- gate_values: float32 [65536, 4], P(('dp', 'ep')), parts along dimension 0, may hold values from 0.1 to 1
- latent_down: bfloat16 [2048, 512], P('ep'), may hold values from -0.125 to 0.125
- latent_up: bfloat16 [512, 2048], P(None, 'ep'), may hold values from -0.25 to 0.25
- expert_up: bfloat16 [128, 512, 1408], P('ep'), may hold values from -0.25 to 0.25
- expert_down: bfloat16 [128, 1408, 512], P('ep'), may hold values from -0.15625 to 0.15625
- grad_out: bfloat16 [65536, 2048], P(('dp', 'ep')), parts along dimension 0, may hold values from -6 to 6
Outputs:
- layer_out: bfloat16 [65536, 2048], P(('dp', 'ep')), parts along dimension 0
- grad_tokens: bfloat16 [65536, 2048], P(('dp', 'ep')), parts along dimension 0
The draws below stay inside these ranges and needn't reach their ends.
There are 4 independent parts, one for each index of `dp`. The reference program is written for one: setup_inputs(seed, part) draws one part's arguments, and reference() takes and returns one part's arrays. A program takes and returns all parts, laid end to end along the dimension named above; an argument that names none is the same for every part. Nothing has to cross between parts.
Inputs may be any that keep to these rules, and one draw needn't show every extreme that they name: `expert_ids`: each row names 4 different experts. Among the 128 tokens of one device, no expert is named by more than 6 tokens, and in every draw some expert is named by exactly 6 tokens of some device.
All inputs are finite; a program needn't handle non-finite values.
Results may differ from the reference program's by a relative error of at most 0.013.
Values may be sent and summed in bfloat16 or wider, within the bound.
No kernel may reach another device: no remote copies, remote signals or barrier semaphores. Data moves between devices by JAX's collectives and lax.ppermute only.
A program may use at most 64 MiB of HBM per device.

```python
import math
import jax
import jax.numpy as jnp
import numpy as np
from jax import lax

D = 2048
L = 512
FF = 1408
TOK_DEV = 128
EXPERTS = 128
TOPK = 4
MOST = 6
TOKENS = 16384
N_EP = 128


def shard_levels(key, shape, split, low, top_value):
    factor_of, own = 1.0, jax.random.fold_in(key, 6)
    for axis_at, parts in split:
        heights = jnp.exp(jax.random.uniform(jax.random.fold_in(own, axis_at), (parts,), jnp.float32, low / len(split), top_value / len(split)))
        factor_of = factor_of * jnp.repeat(heights, shape[axis_at] // parts).reshape([-1 if axis == axis_at else 1 for axis in range(len(shape))])
    return factor_of


def routed_block(own_key, own, number, rows, number_of, top, reach, skew):
    order = jax.random.permutation(own_key, number_of)
    crowded, ordinary = portions_of(number_of, rows * top, reach, skew, True), portions_of(number_of, rows * top, reach, skew, False)
    places = jnp.arange(number_of)

    def named(sizes, turn):
        used = int((sizes > 0).sum())
        fixed = max(1, used // 4)
        shifted = fixed + (places - fixed + turn * (used - fixed)) % max(1, number_of - fixed)
        return jnp.zeros((number_of,), jnp.int32).at[order[jnp.where(places < fixed, places, shifted)]].set(jnp.asarray(sizes, jnp.int32))

    sizes = jnp.where(number % 4 == 0, named(crowded, number // 4), named(ordinary, number - number // 4 - 1))
    mixed = jax.random.permutation(jax.random.fold_in(own, 3), number_of)
    giver, receiver = mixed[0:number_of // 2 * 2:2], mixed[1:number_of // 2 * 2:2]
    slack = jnp.minimum(sizes[giver] - 1, reach - sizes[receiver]) // 2
    slack = jnp.where((giver == order[0]) | (receiver == order[0]) | (sizes[receiver] == 0), 0, jnp.maximum(slack, 0))
    shifted = jax.random.randint(jax.random.fold_in(own, 4), (number_of // 2,), 0, 1 << 20) % (slack + 1)
    sizes = sizes.at[giver].add(-shifted).at[receiver].add(shifted)
    labels = jnp.searchsorted(jnp.cumsum(sizes), jnp.arange(rows * top), side="right").astype(jnp.int32)
    grid = labels.reshape(top, rows).T
    grid = grid[jax.random.permutation(jax.random.fold_in(own, 1), rows)]
    turn = jax.random.randint(jax.random.fold_in(own, 2), (rows, 1), 0, top)
    return jnp.take_along_axis(grid, (jnp.arange(top)[None, :] + turn) % top, axis=1)


def portions_of(amount, total, reach, slope, full):
    loads = [(1 << 20) // math.isqrt(rank ** slope) + 1 for rank in range(1, amount + 1)]
    largest = reach if full else min(reach, max(-(-total // amount), total * loads[0] // sum(loads)))
    least = 1 if total - largest >= amount - 1 else 0
    counts, spare = [largest] + [least] * (amount - 1), total - largest - least * (amount - 1)
    while spare > 0:
        candidates = [i for i in range(1, amount) if counts[i] < largest] or [i for i in range(1, amount) if counts[i] < reach]
        whole, remaining = sum([loads[i] for i in candidates]), spare
        for i in candidates:
            addition = min(reach - counts[i], max(1, remaining * loads[i] // whole), spare)
            counts[i] = counts[i] + addition
            spare = spare - addition
    return np.array(counts)


def gaussian(stream_key, shape, width, bound, split=(), dtype=jnp.bfloat16):
    drawn = jax.random.normal(stream_key, shape, jnp.float32) * width
    if len(split) > 0:
        drawn = shard_levels(stream_key, shape, split, -0.22, 0.18) * drawn
    return jnp.clip(drawn, min=-bound, max=bound).astype(dtype)


def setup_inputs(seed: int = 0, part: int = 0) -> dict:
    seeds = jax.random.split(jax.random.key(seed), 9)
    part_splits = jax.random.split(jax.random.fold_in(seeds[8], part), 9)
    tokens = gaussian(part_splits[0], (TOKENS, D), 1.0, 6.0, ((0, 128),))
    expert_ids_keys = jax.random.split(jax.random.fold_in(part_splits[1], 1), TOKENS // TOK_DEV)
    expert_ids_turns = jax.random.permutation(jax.random.fold_in(part_splits[1], 3), TOKENS // TOK_DEV)
    expert_ids = jax.vmap(lambda own, number: routed_block(jax.random.fold_in(part_splits[1], 2), own, number, TOK_DEV, EXPERTS, TOPK, MOST, 2))(expert_ids_keys, expert_ids_turns).reshape((TOKENS, TOPK))
    gate_values = jnp.clip(jnp.exp(math.log(1.0) - 2.3025851 * jax.random.uniform(part_splits[2], (TOKENS, TOPK), jnp.float32) ** shard_levels(part_splits[2], (TOKENS, TOPK), ((0, 128),), -0.2, 0.2)), 0.1, 1.0)
    latent_down = gaussian(seeds[3], (D, L), D ** -0.5, 0.125, ((0, 128),))
    latent_up = gaussian(seeds[4], (L, D), L ** -0.5, 0.25, ((1, 128),))
    expert_up = gaussian(seeds[5], (EXPERTS, L, FF), L ** -0.5, 0.25, ((0, 128),))
    expert_down = gaussian(seeds[6], (EXPERTS, FF, L), FF ** -0.5, 0.15625, ((0, 128),))
    grad_out = gaussian(part_splits[7], (TOKENS, D), 1.0, 6.0, ((0, 128),))
    return dict(tokens=tokens, expert_ids=expert_ids, gate_values=gate_values, latent_down=latent_down, latent_up=latent_up, expert_up=expert_up, expert_down=expert_down, grad_out=grad_out)


def contract_last(left, right):
    return lax.dot_general(left, right, (((1,), (1,)), ((), ())), preferred_element_type=jnp.float32)


def reference(tokens, expert_ids, gate_values, latent_down, latent_up, expert_up, expert_down, grad_out):
    latent = jnp.dot(tokens, latent_down, preferred_element_type=jnp.float32).astype(jnp.bfloat16)
    grad_latent = contract_last(grad_out, latent_up)
    capacity = N_EP * MOST
    flat_ids = expert_ids.reshape(-1)
    flat_tok = (jnp.arange(flat_ids.shape[0]) // TOPK).astype(jnp.int32)
    flat_gate = gate_values.reshape(-1)
    numbers = jnp.arange(EXPERTS).astype(jnp.int32)
    row_count = tokens.shape[0]

    def per_expert(totals, inputs):
        combined, grad_sum = totals
        expert_num, up_weight, down_weight = inputs
        member = flat_ids == expert_num
        filled = jnp.sum(member.astype(jnp.int32))
        chosen = jnp.nonzero(member, size=capacity, fill_value=0)[0].astype(jnp.int32)
        live_slot = jnp.arange(capacity) < filled
        token_rows = flat_tok[chosen]
        gate_col = jnp.where(live_slot, flat_gate[chosen], jnp.zeros_like(flat_gate[chosen]))[:, None]
        arrived = latent[token_rows]
        pre_act = jnp.dot(arrived, up_weight, preferred_element_type=jnp.float32)
        squared = jnp.square(jax.nn.relu(pre_act)).astype(jnp.bfloat16)
        expert_out = jnp.dot(squared, down_weight, preferred_element_type=jnp.float32).astype(jnp.bfloat16)
        combined = combined.at[token_rows].add(gate_col * expert_out.astype(jnp.float32))
        grad_rows = (gate_col * grad_latent[token_rows]).astype(jnp.bfloat16)
        grad_act = contract_last(grad_rows, down_weight)
        grad_pre = (2.0 * jax.nn.relu(pre_act) * grad_act).astype(jnp.bfloat16)
        grad_in = contract_last(grad_pre, up_weight).astype(jnp.bfloat16).astype(jnp.float32)
        grad_in = jnp.where(live_slot[:, None], grad_in, jnp.zeros_like(grad_in))
        grad_sum = grad_sum.at[token_rows].add(grad_in)
        return (combined, grad_sum), None

    start_totals = (jnp.zeros((row_count, L), jnp.float32), jnp.zeros((row_count, L), jnp.float32))
    (combined, grad_sum), unused = lax.scan(per_expert, start_totals, (numbers, expert_up, expert_down))
    layer_out = jnp.dot(combined.astype(jnp.bfloat16), latent_up, preferred_element_type=jnp.float32).astype(jnp.bfloat16)
    grad_tokens = contract_last(grad_sum.astype(jnp.bfloat16), latent_down).astype(jnp.bfloat16)
    return (layer_out, grad_tokens)
```

```python
import functools

import jax
import jax.numpy as jnp
from jax import lax
from jax.experimental import pallas as pl
from jax.experimental.pallas import tpu as pltpu
from jax.sharding import PartitionSpec as P

SLOTS = 6
LANES = 128
MIB = 2**20


def dot(left, right):
    return jnp.dot(left, right, preferred_element_type=jnp.float32)


def contract_last(left, right):
    return lax.dot_general(
        left, right, (((1,), (1,)), ((), ())), preferred_element_type=jnp.float32
    )


def vmem_call(body, out_shape, scratch, limit_mib, flops, moved):
    return pl.pallas_call(
        body,
        out_shape=out_shape,
        scratch_shapes=scratch,
        compiler_params=pltpu.CompilerParams(vmem_limit_bytes=limit_mib * MIB),
        cost_estimate=pl.CostEstimate(flops=flops, bytes_accessed=moved, transcendentals=0),
    )


def route_kernel(experts, own_ids, other_ids, gates, place_ref, high_ref, low_ref):
    tok = own_ids.shape[1]
    number = lax.broadcasted_iota(jnp.int32, (experts, tok), 0)
    earlier = (
        lax.broadcasted_iota(jnp.int32, (tok, tok), 0)
        < lax.broadcasted_iota(jnp.int32, (tok, tok), 1)
    ).astype(jnp.bfloat16)
    for half, ids in enumerate((own_ids, other_ids)):
        routed = jnp.zeros((experts, tok), jnp.float32)
        weight = jnp.zeros((experts, tok), jnp.float32)
        for k in range(ids.shape[0]):
            named = ids[k : k + 1, :] == number
            routed += jnp.where(named, 1.0, 0.0)
            if half == 0:
                weight += jnp.where(named, gates[k : k + 1, :], 0.0)
        before = dot(routed.astype(jnp.bfloat16), earlier)
        for s in range(SLOTS):
            here = before == float(s)
            place_ref[half * SLOTS + s] = jnp.where(here, routed, 0.0).astype(jnp.bfloat16)
            if half == 0:
                gate = jnp.transpose(jnp.where(here, weight, 0.0))
                high = gate.astype(jnp.bfloat16)
                at = pl.ds(s * experts, experts)
                high_ref[:, at] = high
                low_ref[:, at] = (gate - high.astype(jnp.float32)).astype(jnp.bfloat16)


def whole_weight(w_ref):
    shards, rows, lanes = w_ref.shape
    per = 16
    parts = [
        w_ref[:, j * per : (j + 1) * per, :].reshape(shards * per, lanes)
        for j in range(rows // per)
    ]
    return jnp.concatenate(parts, axis=1)


def send_kernel(experts, own_ref, other_ref, w_ref, place_ref, out_ref, scr):
    tok = own_ref.shape[0]
    weight = whole_weight(w_ref)
    block = out_ref.shape[0] // experts
    for half, x_ref in enumerate((own_ref, other_ref)):
        latent = dot(x_ref[...], weight).astype(jnp.bfloat16)
        for s in range(SLOTS):
            rows = dot(place_ref[half * SLOTS + s], latent)
            for j in range(rows.shape[1] // LANES):
                first = (half * SLOTS + s) * (rows.shape[1] // LANES) + j
                scr[pl.ds(first, experts, stride=block), :] = rows[:, j * LANES : (j + 1) * LANES]
    out_ref[...] = scr[...].astype(jnp.bfloat16)


def expert_kernel(chips, in_ref, up_ref, down_ref, out_ref, scr, lat, grad):
    width = lat.shape[1]
    chunks = width // LANES
    block = 2 * SLOTS * chunks
    scr[...] = in_ref[...].astype(jnp.float32)
    for core in range(2):
        for s in range(SLOTS):
            slot = core * SLOTS + s
            for j in range(chunks):
                at = (pl.ds(slot * chips, chips), pl.ds(j * LANES, LANES))
                first = (core * SLOTS + s) * chunks + j
                lat[at] = scr[pl.ds(first, chips, stride=2 * block), :].astype(jnp.bfloat16)
                first = block + ((1 - core) * SLOTS + s) * chunks + j
                grad[at] = scr[pl.ds(first, chips, stride=2 * block), :].astype(jnp.bfloat16)
    per = lat.shape[0] // 3
    slots_per = per // chips
    for m in range(3):
        at = pl.ds(m * per, per)
        act = jnp.maximum(dot(lat[at, :], up_ref[...]), 0.0)
        squared = jnp.square(act).astype(jnp.bfloat16)
        out = dot(squared, down_ref[...])
        grad_act = contract_last(grad[at, :], down_ref[...])
        grad_pre = (2.0 * act * grad_act).astype(jnp.bfloat16)
        back = contract_last(grad_pre, up_ref[...])
        for q in range(slots_per):
            core, s = divmod(m * slots_per + q, SLOTS)
            for j in range(chunks):
                part = (slice(q * chips, (q + 1) * chips), slice(j * LANES, (j + 1) * LANES))
                first = core * block + s * chunks + j
                scr[pl.ds(first, chips, stride=2 * block), :] = out[part]
                scr[pl.ds(first + block // 2, chips, stride=2 * block), :] = back[part]
    out_ref[...] = scr[...].astype(jnp.bfloat16)


def finish_kernel(
    experts, core_ref, in_ref, high_ref, low_ref, mine_ref, other_ref, layer_ref, grad_ref, scr, rows
):
    chunks = rows.shape[1] // (2 * LANES)
    block = 2 * SLOTS * chunks
    scr[...] = in_ref[...].astype(jnp.float32)
    for s in range(SLOTS):
        for kind in range(2):
            for j in range(chunks):
                first = (kind * SLOTS + s) * chunks + j
                at = (pl.ds(s * experts, experts), pl.ds((kind * chunks + j) * LANES, LANES))
                rows[at] = scr[pl.ds(first, experts, stride=block), :].astype(jnp.bfloat16)
    total = dot(high_ref[...], rows[...]) + dot(low_ref[...], rows[...])
    total = total.astype(jnp.bfloat16)
    width = chunks * LANES
    combined, grad_sum = total[:, :width], total[:, width:]
    even = core_ref[0] == 0
    mine = contract_last(jnp.where(even, grad_sum, combined), whole_weight(mine_ref))
    other = contract_last(jnp.where(even, combined, grad_sum), whole_weight(other_ref))
    layer_ref[...] = jnp.where(even, other, mine).astype(jnp.bfloat16)
    grad_ref[...] = jnp.where(even, mine, other).astype(jnp.bfloat16)


def on_device(tokens, expert_ids, gate_values, latent_down, latent_up, expert_up, expert_down, grad_out):
    ep = lax.axis_size("ep")
    tok, wide = tokens.shape
    shard, width = latent_down.shape
    hidden = expert_up.shape[2]
    chunks = width // LANES
    block = 2 * SLOTS * chunks
    core = lax.axis_index("ep") % 2
    swap = [(i, i ^ 1) for i in range(ep)]
    bf16, f32 = jnp.bfloat16, jnp.float32

    def chunked(rows):
        return rows.reshape(shard, chunks, LANES).transpose(1, 0, 2).reshape(chunks * shard, LANES)

    both = jnp.stack([chunked(latent_down), chunked(latent_up.T)])
    cast = jnp.broadcast_to(both[None], (ep // 2, 2, chunks * shard, LANES))
    role = lax.all_to_all(
        cast.reshape(ep, chunks * shard, LANES), "ep", split_axis=0, concat_axis=0, tiled=True
    )

    even = core == 0
    own = jnp.where(even, tokens, grad_out)
    other = lax.ppermute(jnp.where(even, grad_out, tokens), "ep", swap)
    own_ids = expert_ids.T
    other_ids = lax.ppermute(own_ids, "ep", swap)

    place, high, low = vmem_call(
        functools.partial(route_kernel, ep),
        (
            jax.ShapeDtypeStruct((2 * SLOTS, ep, tok), bf16),
            jax.ShapeDtypeStruct((tok, SLOTS * ep), bf16),
            jax.ShapeDtypeStruct((tok, SLOTS * ep), bf16),
        ),
        [],
        8,
        4 * tok * tok * ep,
        MIB,
    )(own_ids, other_ids, gate_values.T)

    outbound = vmem_call(
        functools.partial(send_kernel, ep),
        jax.ShapeDtypeStruct((ep * block, LANES), bf16),
        [pltpu.VMEM((ep * block, LANES), f32)],
        24,
        4 * tok * wide * width,
        6 * MIB,
    )(own, other, role, place)

    arrived = lax.all_to_all(
        outbound.reshape(ep, block, LANES), "ep", split_axis=0, concat_axis=0, tiled=True
    )
    role_other = lax.ppermute(role, "ep", swap)

    rows = ep // 2 * 2 * SLOTS
    done = vmem_call(
        functools.partial(expert_kernel, ep // 2),
        jax.ShapeDtypeStruct((ep * block, LANES), bf16),
        [
            pltpu.VMEM((ep * block, LANES), f32),
            pltpu.VMEM((rows, width), bf16),
            pltpu.VMEM((rows, width), bf16),
        ],
        40,
        8 * rows * width * hidden,
        8 * MIB,
    )(arrived.reshape(ep * block, LANES), expert_up[0], expert_down[0])

    returned = lax.all_to_all(
        done.reshape(ep, block, LANES), "ep", split_axis=0, concat_axis=0, tiled=True
    )
    return pl.pallas_call(
        functools.partial(finish_kernel, ep),
        out_shape=(
            jax.ShapeDtypeStruct((tok, wide), bf16),
            jax.ShapeDtypeStruct((tok, wide), bf16),
        ),
        in_specs=[pl.BlockSpec(memory_space=pltpu.SMEM)]
        + [pl.BlockSpec(memory_space=pltpu.VMEM)] * 5,
        scratch_shapes=[
            pltpu.VMEM((ep * block, LANES), f32),
            pltpu.VMEM((SLOTS * ep, 2 * width), bf16),
        ],
        compiler_params=pltpu.CompilerParams(vmem_limit_bytes=32 * MIB),
        cost_estimate=pl.CostEstimate(
            flops=4 * tok * wide * width, bytes_accessed=7 * MIB, transcendentals=0
        ),
    )(core.reshape(1).astype(jnp.int32), returned.reshape(ep * block, LANES), high, low, role, role_other)


def solution(mesh):
    rows = P(("dp", "ep"), None)
    experts = P("ep", None, None)
    return jax.shard_map(
        on_device,
        mesh=mesh,
        in_specs=(rows, rows, rows, P("ep", None), P(None, "ep"), experts, experts, rows),
        out_specs=(rows, rows),
        check_vma=False,
    )
```

```python
import functools

import jax
import jax.numpy as jnp
from jax import lax
from jax.experimental import pallas as pl
from jax.experimental.pallas import tpu as pltpu
from jax.sharding import PartitionSpec as P

SLOTS = 6
LANES = 128
MIB = 2**20


def dot(left, right):
    return jnp.dot(left, right, preferred_element_type=jnp.float32)


def contract_last(left, right):
    return lax.dot_general(
        left, right, (((1,), (1,)), ((), ())), preferred_element_type=jnp.float32
    )


def vmem_call(body, out_shape, scratch, limit_mib, flops, moved, arrays, scalars=0):
    return pl.pallas_call(
        body,
        out_shape=out_shape,
        in_specs=[pl.BlockSpec(memory_space=pltpu.SMEM)] * scalars
        + [pl.BlockSpec(memory_space=pltpu.VMEM)] * arrays,
        scratch_shapes=scratch,
        compiler_params=pltpu.CompilerParams(vmem_limit_bytes=limit_mib * MIB),
        cost_estimate=pl.CostEstimate(flops=flops, bytes_accessed=moved, transcendentals=0),
    )


def route_kernel(experts, own_ids, other_ids, gates, place_ref, high_ref, low_ref):
    tok = own_ids.shape[1]
    number = lax.broadcasted_iota(jnp.int32, (experts, tok), 0)
    earlier = (
        lax.broadcasted_iota(jnp.int32, (tok, tok), 0)
        < lax.broadcasted_iota(jnp.int32, (tok, tok), 1)
    ).astype(jnp.bfloat16)
    for half, ids in enumerate((own_ids, other_ids)):
        routed = jnp.zeros((experts, tok), jnp.float32)
        weight = jnp.zeros((experts, tok), jnp.float32)
        for k in range(ids.shape[0]):
            named = ids[k : k + 1, :] == number
            routed += jnp.where(named, 1.0, 0.0)
            if half == 0:
                weight += jnp.where(named, gates[k : k + 1, :], 0.0)
        before = dot(routed.astype(jnp.bfloat16), earlier)
        for s in range(SLOTS):
            here = before == float(s)
            place_ref[half * SLOTS + s] = jnp.where(here, routed, 0.0).astype(jnp.bfloat16)
            if half == 0:
                gate = jnp.transpose(jnp.where(here, weight, 0.0))
                high = gate.astype(jnp.bfloat16)
                at = pl.ds(s * experts, experts)
                high_ref[:, at] = high
                low_ref[:, at] = (gate - high.astype(jnp.float32)).astype(jnp.bfloat16)


def cast_kernel(plane_ref, down_ref, up_ref, out_ref):
    shard = jnp.where(plane_ref[0] == 0, down_ref[...], up_ref[...])
    rows, width = shard.shape
    for j in range(width // LANES):
        piece = shard[:, j * LANES : (j + 1) * LANES]
        at = pl.ds(j * rows, rows)
        out_ref[:, at, :] = jnp.broadcast_to(piece[None], (out_ref.shape[0], rows, LANES))


def half_weight(w_ref):
    shards, rows, lanes = w_ref.shape
    per = 16
    parts = [
        w_ref[:, j * per : (j + 1) * per, :].reshape(shards * per, lanes)
        for j in range(rows // per)
    ]
    return jnp.concatenate(parts, axis=1)


def project_kernel(a_ref, b_ref, c_ref, d_ref, w_ref, mine_ref, theirs_ref):
    weight = half_weight(w_ref)
    tok = a_ref.shape[0]
    for n, x_ref in enumerate((a_ref, b_ref, c_ref, d_ref)):
        out_ref = (mine_ref, theirs_ref)[n // 2]
        out_ref[pl.ds(n % 2 * tok, tok), :] = dot(x_ref[...], weight).astype(jnp.bfloat16)


def send_kernel(experts, plane_ref, mine_ref, swapped_ref, place_ref, out_ref, scr):
    first_plane = plane_ref[0] == 0
    mine, swapped = mine_ref[...], swapped_ref[...]
    latent = jnp.where(first_plane, mine, swapped)
    grad = jnp.where(first_plane, swapped, mine)
    both = jnp.concatenate([latent, grad], axis=1)
    tok = both.shape[0] // 2
    chunks = both.shape[1] // LANES
    block = 2 * SLOTS * chunks
    for half in range(2):
        for s in range(SLOTS):
            rows = dot(place_ref[half * SLOTS + s], both[half * tok : (half + 1) * tok])
            for j in range(chunks):
                first = (half * SLOTS + s) * chunks + j
                scr[pl.ds(first, experts, stride=block), :] = rows[:, j * LANES : (j + 1) * LANES]
    out_ref[...] = scr[...].astype(jnp.bfloat16)


def expert_kernel(chips, in_ref, up_ref, down_ref, out_ref, scr, lat, grad):
    width = lat.shape[1]
    chunks = width // LANES
    block = 2 * SLOTS * chunks
    scr[...] = in_ref[...].astype(jnp.float32)
    for core in range(2):
        for s in range(SLOTS):
            for j in range(chunks):
                sender, part = divmod(j, chunks // 2)
                slot = s if sender == core else SLOTS + s
                at = (pl.ds((core * SLOTS + s) * chips, chips), pl.ds(j * LANES, LANES))
                first = sender * block + slot * chunks + part
                lat[at] = scr[pl.ds(first, chips, stride=2 * block), :].astype(jnp.bfloat16)
                first += chunks // 2
                grad[at] = scr[pl.ds(first, chips, stride=2 * block), :].astype(jnp.bfloat16)
    per = lat.shape[0] // 3
    slots_per = per // chips
    for m in range(3):
        at = pl.ds(m * per, per)
        act = jnp.maximum(dot(lat[at, :], up_ref[...]), 0.0)
        squared = jnp.square(act).astype(jnp.bfloat16)
        out = dot(squared, down_ref[...])
        grad_act = contract_last(grad[at, :], down_ref[...])
        grad_pre = (2.0 * act * grad_act).astype(jnp.bfloat16)
        back = contract_last(grad_pre, up_ref[...])
        for q in range(slots_per):
            core, s = divmod(m * slots_per + q, SLOTS)
            for j in range(chunks):
                part = (slice(q * chips, (q + 1) * chips), slice(j * LANES, (j + 1) * LANES))
                first = core * block + s * chunks + j
                scr[pl.ds(first, chips, stride=2 * block), :] = out[part]
                scr[pl.ds(first + block // 2, chips, stride=2 * block), :] = back[part]
    out_ref[...] = scr[...].astype(jnp.bfloat16)


def weight_kernel(place_ref, same_ref, next_ref, plane_ref, far_ref, down_ref, up_ref):
    first_plane, first_core = place_ref[0] == 0, place_ref[1] == 0
    half = down_ref.shape[1] // 2
    per = 16
    for j in range(half // LANES):
        rows = slice(j * per, (j + 1) * per)

        def piece(ref):
            return ref[:, rows, :].reshape(-1, LANES)

        same, beside, plane, far = piece(same_ref), piece(next_ref), piece(plane_ref), piece(far_ref)
        for low in range(2):
            mine = jnp.where(first_core, (same, beside)[low], (beside, same)[low])
            theirs = jnp.where(first_core, (plane, far)[low], (far, plane)[low])
            at = pl.ds(low * half + j * LANES, LANES)
            down_ref[:, at] = jnp.where(first_plane, mine, theirs)
            up_ref[:, at] = jnp.where(first_plane, theirs, mine)


def finish_kernel(experts, in_ref, high_ref, low_ref, down_ref, up_ref, layer_ref, grad_ref, scr, rows):
    chunks = rows.shape[1] // (2 * LANES)
    block = 2 * SLOTS * chunks
    scr[...] = in_ref[...].astype(jnp.float32)
    for s in range(SLOTS):
        for kind in range(2):
            for j in range(chunks):
                first = (kind * SLOTS + s) * chunks + j
                at = (pl.ds(s * experts, experts), pl.ds((kind * chunks + j) * LANES, LANES))
                rows[at] = scr[pl.ds(first, experts, stride=block), :].astype(jnp.bfloat16)
    total = dot(high_ref[...], rows[...]) + dot(low_ref[...], rows[...])
    total = total.astype(jnp.bfloat16)
    width = chunks * LANES
    layer_ref[...] = contract_last(total[:, :width], up_ref[...]).astype(jnp.bfloat16)
    grad_ref[...] = contract_last(total[:, width:], down_ref[...]).astype(jnp.bfloat16)


def on_device(tokens, expert_ids, gate_values, latent_down, latent_up, expert_up, expert_down, grad_out):
    ep, dp = lax.axis_size("ep"), lax.axis_size("dp")
    tok, wide = tokens.shape
    shard, width = latent_down.shape
    hidden = expert_up.shape[2]
    chunks = width // LANES
    block = 2 * SLOTS * chunks
    core = (lax.axis_index("ep") % 2).astype(jnp.int32)
    plane = (lax.axis_index("dp") % 2).astype(jnp.int32)
    place_of = jnp.stack([plane, core])
    bf16, f32 = jnp.bfloat16, jnp.float32

    def beside(x):
        return lax.ppermute(x, "ep", [(i, i ^ 1) for i in range(ep)])

    def next_plane(x):
        return lax.ppermute(x, "dp", [(i, i ^ 1) for i in range(dp)])

    def exchange(x):
        return lax.all_to_all(x, "ep", split_axis=0, concat_axis=0, tiled=True)

    cast = vmem_call(
        cast_kernel,
        jax.ShapeDtypeStruct((ep // 2, chunks * shard, LANES), bf16),
        [],
        8,
        0,
        MIB,
        scalars=1,
        arrays=2,
    )(place_of, latent_down, latent_up.T)
    same = exchange(cast.reshape(ep, chunks // 2 * shard, LANES))

    first_plane = plane == 0
    own = jnp.where(first_plane, tokens, grad_out)
    theirs = next_plane(jnp.where(first_plane, grad_out, tokens))
    own_ids = expert_ids.T

    place, high, low = vmem_call(
        functools.partial(route_kernel, ep),
        (
            jax.ShapeDtypeStruct((2 * SLOTS, ep, tok), bf16),
            jax.ShapeDtypeStruct((tok, SLOTS * ep), bf16),
            jax.ShapeDtypeStruct((tok, SLOTS * ep), bf16),
        ),
        [],
        8,
        4 * tok * tok * ep,
        MIB,
        arrays=3,
    )(own_ids, beside(own_ids), gate_values.T)

    projected = jax.ShapeDtypeStruct((2 * tok, width // 2), bf16)
    mine, away = vmem_call(
        project_kernel,
        (projected, projected),
        [],
        12,
        4 * tok * wide * width,
        4 * MIB,
        arrays=5,
    )(own, beside(own), theirs, beside(theirs), same)

    outbound = vmem_call(
        functools.partial(send_kernel, ep),
        jax.ShapeDtypeStruct((ep * block, LANES), bf16),
        [pltpu.VMEM((ep * block, LANES), f32)],
        12,
        4 * SLOTS * tok * ep * width,
        3 * MIB,
        scalars=1,
        arrays=3,
    )(place_of, mine, next_plane(away), place)

    arrived = exchange(outbound.reshape(ep, block, LANES))
    other = next_plane(same)

    rows = ep // 2 * 2 * SLOTS
    done = vmem_call(
        functools.partial(expert_kernel, ep // 2),
        jax.ShapeDtypeStruct((ep * block, LANES), bf16),
        [
            pltpu.VMEM((ep * block, LANES), f32),
            pltpu.VMEM((rows, width), bf16),
            pltpu.VMEM((rows, width), bf16),
        ],
        32,
        8 * rows * width * hidden,
        8 * MIB,
        arrays=3,
    )(arrived.reshape(ep * block, LANES), expert_up[0], expert_down[0])

    returned = exchange(done.reshape(ep, block, LANES))
    whole = jax.ShapeDtypeStruct((wide, width), bf16)
    down, up = vmem_call(
        weight_kernel, (whole, whole), [], 16, 0, 8 * MIB, scalars=1, arrays=4
    )(place_of, same, beside(same), other, beside(other))
    result = jax.ShapeDtypeStruct((tok, wide), bf16)
    return vmem_call(
        functools.partial(finish_kernel, ep),
        (result, result),
        [
            pltpu.VMEM((ep * block, LANES), f32),
            pltpu.VMEM((SLOTS * ep, 2 * width), bf16),
        ],
        20,
        4 * tok * wide * width,
        7 * MIB,
        arrays=5,
    )(returned.reshape(ep * block, LANES), high, low, down, up)


def solution(mesh):
    rows = P(("dp", "ep"), None)
    experts = P("ep", None, None)
    return jax.shard_map(
        on_device,
        mesh=mesh,
        in_specs=(rows, rows, rows, P("ep", None), P(None, "ep"), experts, experts, rows),
        out_specs=(rows, rows),
        check_vma=False,
    )
```

```python
import functools

import jax
import jax.numpy as jnp
from jax import lax
from jax.experimental import pallas as pl
from jax.experimental.pallas import tpu as pltpu
from jax.sharding import PartitionSpec as P

SLOTS = 6
PITCH = 136
LANES = 128
MIB = 2**20


def dot(left, right):
    return jnp.dot(left, right, preferred_element_type=jnp.float32)


def contract_last(left, right):
    return lax.dot_general(
        left, right, (((1,), (1,)), ((), ())), preferred_element_type=jnp.float32
    )


def vmem_call(body, out_shape, scratch, limit_mib, flops, moved, arrays, scalars=0, far=0, far_out=False):
    return pl.pallas_call(
        body,
        out_shape=out_shape,
        in_specs=[pl.BlockSpec(memory_space=pltpu.SMEM)] * scalars
        + [pl.BlockSpec(memory_space=pltpu.VMEM)] * arrays
        + [pl.BlockSpec(memory_space=pl.ANY)] * far,
        **({"out_specs": pl.BlockSpec(memory_space=pltpu.HBM)} if far_out else {}),
        scratch_shapes=scratch,
        compiler_params=pltpu.CompilerParams(vmem_limit_bytes=limit_mib * MIB),
        cost_estimate=pl.CostEstimate(flops=flops, bytes_accessed=moved, transcendentals=0),
    )


def route_kernel(experts, own_ids, other_ids, gates, place_ref, high_ref, low_ref):
    tok = own_ids.shape[1]
    number = lax.broadcasted_iota(jnp.int32, (experts, tok), 0)
    earlier = (
        lax.broadcasted_iota(jnp.int32, (tok, tok), 0)
        < lax.broadcasted_iota(jnp.int32, (tok, tok), 1)
    ).astype(jnp.bfloat16)
    for half, ids in enumerate((own_ids, other_ids)):
        routed = jnp.zeros((experts, tok), jnp.float32)
        weight = jnp.zeros((experts, tok), jnp.float32)
        for k in range(ids.shape[0]):
            named = ids[k : k + 1, :] == number
            routed += jnp.where(named, 1.0, 0.0)
            if half == 0:
                weight += jnp.where(named, gates[k : k + 1, :], 0.0)
        before = dot(routed.astype(jnp.bfloat16), earlier)
        for s in range(SLOTS):
            here = before == float(s)
            place_ref[half * SLOTS + s] = jnp.where(here, routed, 0.0).astype(jnp.bfloat16)
            if half == 0:
                gate = jnp.transpose(jnp.where(here, weight, 0.0))
                high = gate.astype(jnp.bfloat16)
                at = pl.ds(s * experts, experts)
                high_ref[:, at] = high
                low_ref[:, at] = (gate - high.astype(jnp.float32)).astype(jnp.bfloat16)


def cast_kernel(plane_ref, down_ref, up_ref, out_ref, shard, piece, in_sem, out_sem):
    @pl.when(plane_ref[0] == 0)
    def _():
        pltpu.make_async_copy(down_ref, shard, in_sem).start()

    @pl.when(plane_ref[0] != 0)
    def _():
        pltpu.make_async_copy(up_ref, shard, in_sem).start()

    pltpu.make_async_copy(down_ref, shard, in_sem).wait()
    rows, width = shard.shape
    for j in range(width // LANES):
        chunk = shard[:, j * LANES : (j + 1) * LANES]
        piece[:, pl.ds(j * rows, rows), :] = jnp.broadcast_to(chunk[None], (piece.shape[0], rows, LANES))
    count = piece.shape[0]
    copies = [
        pltpu.make_async_copy(piece, out_ref.at[pl.ds(n * count, count)], out_sem.at[n])
        for n in range(out_ref.shape[0] // count)
    ]
    for copy in copies:
        copy.start()
    for copy in copies:
        copy.wait()


def half_weight(w_ref):
    shards, rows, lanes = w_ref.shape
    per = 16
    parts = [
        w_ref[:, j * per : (j + 1) * per, :].reshape(shards * per, lanes)
        for j in range(rows // per)
    ]
    return jnp.concatenate(parts, axis=1)


def project_kernel(a_ref, b_ref, c_ref, d_ref, w_ref, mine_ref, theirs_ref):
    weight = half_weight(w_ref)
    tok = a_ref.shape[0]
    for n, x_ref in enumerate((a_ref, b_ref, c_ref, d_ref)):
        out_ref = (mine_ref, theirs_ref)[n // 2]
        out_ref[pl.ds(n % 2 * tok, tok), :] = dot(x_ref[...], weight).astype(jnp.bfloat16)


def send_kernel(experts, plane_ref, mine_ref, swapped_ref, place_ref, out_ref, scr):
    first_plane = plane_ref[0] == 0
    mine, swapped = mine_ref[...], swapped_ref[...]
    latent = jnp.where(first_plane, mine, swapped)
    grad = jnp.where(first_plane, swapped, mine)
    both = jnp.concatenate([latent, grad], axis=1)
    tok = both.shape[0] // 2
    chunks = both.shape[1] // LANES
    block = 2 * SLOTS * chunks
    for half in range(2):
        for s in range(SLOTS):
            rows = dot(place_ref[half * SLOTS + s], both[half * tok : (half + 1) * tok])
            for j in range(chunks):
                first = ((half * SLOTS + s) * chunks + j) * PITCH
                scr[pl.ds(first, experts), :] = rows[:, j * LANES : (j + 1) * LANES]
    for e in range(experts):
        out_ref[pl.ds(e * block, block), :] = scr[pl.ds(e, block, stride=PITCH), :].astype(jnp.bfloat16)


def expert_kernel(chips, in_ref, up_ref, down_ref, out_ref, scr, lat, grad, made, done, sems):
    width = lat.shape[1]
    chunks = width // LANES
    block = 2 * SLOTS * chunks
    scr[...] = in_ref[...].astype(jnp.float32)
    for core in range(2):
        for s in range(SLOTS):
            for j in range(chunks):
                sender, part = divmod(j, chunks // 2)
                slot = s if sender == core else SLOTS + s
                at = (pl.ds((core * SLOTS + s) * chips, chips), pl.ds(j * LANES, LANES))
                first = sender * block + slot * chunks + part
                lat[at] = scr[pl.ds(first, chips, stride=2 * block), :].astype(jnp.bfloat16)
                first += chunks // 2
                grad[at] = scr[pl.ds(first, chips, stride=2 * block), :].astype(jnp.bfloat16)
    tiles = 2
    per = lat.shape[0] // tiles
    slots_per = per // chips
    for m in range(tiles):
        at = pl.ds(m * per, per)
        act = jnp.maximum(dot(lat[at, :], up_ref[...]), 0.0)
        squared = jnp.square(act).astype(jnp.bfloat16)
        out = dot(squared, down_ref[...])
        grad_act = contract_last(grad[at, :], down_ref[...])
        grad_pre = (2.0 * act * grad_act).astype(jnp.bfloat16)
        back = contract_last(grad_pre, up_ref[...])
        for q in range(slots_per):
            core, s = divmod(m * slots_per + q, SLOTS)
            for j in range(chunks):
                part = (slice(q * chips, (q + 1) * chips), slice(j * LANES, (j + 1) * LANES))
                first = (s * chunks + j) * PITCH + core * chips
                made[pl.ds(first, chips), :] = out[part]
                made[pl.ds(first + block // 2 * PITCH, chips), :] = back[part]
    parts = sems.shape[0]
    copies = []
    for n in range(parts):
        for chip in range(n * chips // parts, (n + 1) * chips // parts):
            for core in range(2):
                rows = made[pl.ds(core * chips + chip, block, stride=PITCH), :]
                done[pl.ds((2 * chip + core) * block, block), :] = rows.astype(jnp.bfloat16)
        at = pl.ds(n * (2 * chips * block // parts), 2 * chips * block // parts)
        copies.append(pltpu.make_async_copy(done.at[at], out_ref.at[at], sems.at[n]))
        copies[-1].start()
    for copy in copies:
        copy.wait()


def finish_kernel(
    experts, place_ref, in_ref, high_ref, low_ref, same_ref, next_ref, plane_ref, far_ref, layer_ref, grad_ref, scr, rows
):
    chunks = rows.shape[1] // (2 * LANES)
    block = 2 * SLOTS * chunks
    scr[...] = in_ref[...].astype(jnp.float32)
    for s in range(SLOTS):
        for kind in range(2):
            for j in range(chunks):
                first = (kind * SLOTS + s) * chunks + j
                at = (pl.ds(s * experts, experts), pl.ds((kind * chunks + j) * LANES, LANES))
                rows[at] = scr[pl.ds(first, experts, stride=block), :].astype(jnp.bfloat16)
    total = dot(high_ref[...], rows[...]) + dot(low_ref[...], rows[...])
    total = total.astype(jnp.bfloat16)
    first_plane, first_core = place_ref[0] == 0, place_ref[1] == 0
    half = chunks * LANES // 2

    def swapped(yes, x):
        return jnp.concatenate(
            [jnp.where(yes, x[:, :half], x[:, half:]), jnp.where(yes, x[:, half:], x[:, :half])], axis=1
        )

    combined = swapped(first_core, total[:, : 2 * half])
    grad_sum = swapped(first_core, total[:, 2 * half :])
    mine = jnp.where(first_plane, grad_sum, combined)
    theirs = jnp.where(first_plane, combined, grad_sum)

    def project(x, this, that):
        return contract_last(x, jnp.concatenate([half_weight(this), half_weight(that)], axis=1))

    mine = project(mine, same_ref, next_ref)
    theirs = project(theirs, plane_ref, far_ref)
    layer_ref[...] = jnp.where(first_plane, theirs, mine).astype(jnp.bfloat16)
    grad_ref[...] = jnp.where(first_plane, mine, theirs).astype(jnp.bfloat16)


def on_device(tokens, expert_ids, gate_values, latent_down, latent_up, expert_up, expert_down, grad_out):
    ep, dp = lax.axis_size("ep"), lax.axis_size("dp")
    tok, wide = tokens.shape
    shard, width = latent_down.shape
    hidden = expert_up.shape[2]
    chunks = width // LANES
    block = 2 * SLOTS * chunks
    core = (lax.axis_index("ep") % 2).astype(jnp.int32)
    plane = (lax.axis_index("dp") % 2).astype(jnp.int32)
    place_of = jnp.stack([plane, core])
    bf16, f32 = jnp.bfloat16, jnp.float32

    def beside(x):
        return lax.ppermute(x, "ep", [(i, i ^ 1) for i in range(ep)])

    def next_plane(x):
        return lax.ppermute(x, "dp", [(i, i ^ 1) for i in range(dp)])

    def exchange(x):
        return lax.all_to_all(x, "ep", split_axis=0, concat_axis=0, tiled=True)

    cast = vmem_call(
        cast_kernel,
        jax.ShapeDtypeStruct((ep // 2, chunks * shard, LANES), bf16),
        [
            pltpu.VMEM((shard, width), bf16),
            pltpu.VMEM((ep // 8, chunks * shard, LANES), bf16),
            pltpu.SemaphoreType.DMA,
            pltpu.SemaphoreType.DMA((4,)),
        ],
        61,
        0,
        MIB,
        arrays=0,
        scalars=1,
        far=2,
        far_out=True,
    )(place_of, latent_down, latent_up.T)
    same = exchange(cast.reshape(ep, chunks // 2 * shard, LANES))

    first_plane = plane == 0
    own = jnp.where(first_plane, tokens, grad_out)
    theirs = next_plane(jnp.where(first_plane, grad_out, tokens))
    own_ids = expert_ids.T

    place, high, low = vmem_call(
        functools.partial(route_kernel, ep),
        (
            jax.ShapeDtypeStruct((2 * SLOTS, ep, tok), bf16),
            jax.ShapeDtypeStruct((tok, SLOTS * ep), bf16),
            jax.ShapeDtypeStruct((tok, SLOTS * ep), bf16),
        ),
        [],
        8,
        4 * tok * tok * ep,
        MIB,
        arrays=3,
    )(own_ids, beside(own_ids), gate_values.T)

    projected = jax.ShapeDtypeStruct((2 * tok, width // 2), bf16)
    mine, away = vmem_call(
        project_kernel,
        (projected, projected),
        [],
        12,
        4 * tok * wide * width,
        4 * MIB,
        arrays=5,
    )(own, beside(own), theirs, beside(theirs), same)

    outbound = vmem_call(
        functools.partial(send_kernel, ep),
        jax.ShapeDtypeStruct((ep * block, LANES), bf16),
        [pltpu.VMEM((block * PITCH, LANES), f32)],
        12,
        4 * SLOTS * tok * ep * width,
        3 * MIB,
        scalars=1,
        arrays=3,
    )(place_of, mine, next_plane(away), place)

    arrived = exchange(outbound.reshape(ep, block, LANES))
    other = next_plane(same)

    rows = ep // 2 * 2 * SLOTS
    done = vmem_call(
        functools.partial(expert_kernel, ep // 2),
        jax.ShapeDtypeStruct((ep * block, LANES), bf16),
        [
            pltpu.VMEM((ep * block, LANES), f32),
            pltpu.VMEM((rows, width), bf16),
            pltpu.VMEM((rows, width), bf16),
            pltpu.VMEM((block * PITCH, LANES), f32),
            pltpu.VMEM((ep * block, LANES), bf16),
            pltpu.SemaphoreType.DMA((4,)),
        ],
        36,
        8 * rows * width * hidden,
        8 * MIB,
        arrays=3,
        far_out=True,
    )(arrived.reshape(ep * block, LANES), expert_up[0], expert_down[0])

    returned = exchange(done.reshape(ep, block, LANES))
    result = jax.ShapeDtypeStruct((tok, wide), bf16)
    return vmem_call(
        functools.partial(finish_kernel, ep),
        (result, result),
        [
            pltpu.VMEM((ep * block, LANES), f32),
            pltpu.VMEM((SLOTS * ep, 2 * width), bf16),
        ],
        51,
        4 * tok * wide * width,
        7 * MIB,
        arrays=7,
        scalars=1,
    )(place_of, returned.reshape(ep * block, LANES), high, low, same, beside(same), other, beside(other))


def solution(mesh):
    rows = P(("dp", "ep"), None)
    experts = P("ep", None, None)
    return jax.shard_map(
        on_device,
        mesh=mesh,
        in_specs=(rows, rows, rows, P("ep", None), P(None, "ep"), experts, experts, rows),
        out_specs=(rows, rows),
        check_vma=False,
    )
```

```python
import functools

import jax
import jax.numpy as jnp
from jax import lax
from jax.experimental import pallas as pl
from jax.experimental.pallas import tpu as pltpu
from jax.sharding import PartitionSpec as P

SLOTS = 6
PITCH = 136
LANES = 128
MIB = 2**20


def dot(left, right):
    return jnp.dot(left, right, preferred_element_type=jnp.float32)


def contract_last(left, right):
    return lax.dot_general(
        left, right, (((1,), (1,)), ((), ())), preferred_element_type=jnp.float32
    )


def vmem_call(body, out_shape, scratch, limit_mib, flops, moved, arrays, far=0, far_out=False):
    return pl.pallas_call(
        body,
        out_shape=out_shape,
        in_specs=[pl.BlockSpec(memory_space=pltpu.VMEM)] * arrays
        + [pl.BlockSpec(memory_space=pl.ANY)] * far,
        **({"out_specs": pl.BlockSpec(memory_space=pltpu.HBM)} if far_out else {}),
        scratch_shapes=scratch,
        compiler_params=pltpu.CompilerParams(vmem_limit_bytes=limit_mib * MIB),
        cost_estimate=pl.CostEstimate(flops=flops, bytes_accessed=moved, transcendentals=0),
    )


def route_kernel(experts, own_ids, other_ids, gates, place_ref, high_ref, low_ref):
    tok = own_ids.shape[1]
    number = lax.broadcasted_iota(jnp.int32, (experts, tok), 0)
    earlier = (
        lax.broadcasted_iota(jnp.int32, (tok, tok), 0)
        < lax.broadcasted_iota(jnp.int32, (tok, tok), 1)
    ).astype(jnp.bfloat16)
    for half, ids in enumerate((own_ids, other_ids)):
        routed = jnp.zeros((experts, tok), jnp.float32)
        weight = jnp.zeros((experts, tok), jnp.float32)
        for k in range(ids.shape[0]):
            named = ids[k : k + 1, :] == number
            routed += jnp.where(named, 1.0, 0.0)
            if half == 0:
                weight += jnp.where(named, gates[k : k + 1, :], 0.0)
        before = dot(routed.astype(jnp.bfloat16), earlier)
        for s in range(SLOTS):
            here = before == float(s)
            place_ref[half * SLOTS + s] = jnp.where(here, routed, 0.0).astype(jnp.bfloat16)
            if half == 0:
                gate = jnp.transpose(jnp.where(here, weight, 0.0))
                high = gate.astype(jnp.bfloat16)
                at = pl.ds(s * experts, experts)
                high_ref[:, at] = high
                low_ref[:, at] = (gate - high.astype(jnp.float32)).astype(jnp.bfloat16)


def cast_kernel(down_ref, up_ref, out_ref, shard, piece, in_sem, out_sem):
    first_plane = lax.axis_index("dp") % 2 == 0

    @pl.when(first_plane)
    def _():
        pltpu.make_async_copy(down_ref, shard, in_sem).start()

    @pl.when(jnp.logical_not(first_plane))
    def _():
        pltpu.make_async_copy(up_ref, shard, in_sem).start()

    pltpu.make_async_copy(down_ref, shard, in_sem).wait()
    rows, width = shard.shape
    for j in range(width // LANES):
        chunk = shard[:, j * LANES : (j + 1) * LANES]
        piece[:, pl.ds(j * rows, rows), :] = jnp.broadcast_to(chunk[None], (piece.shape[0], rows, LANES))
    count = piece.shape[0]
    copies = [
        pltpu.make_async_copy(piece, out_ref.at[pl.ds(n * count, count)], out_sem.at[n])
        for n in range(out_ref.shape[0] // count)
    ]
    for copy in copies:
        copy.start()
    for copy in copies:
        copy.wait()


def half_weight(w_ref):
    shards, rows, lanes = w_ref.shape
    per = 16
    parts = [
        w_ref[:, j * per : (j + 1) * per, :].reshape(shards * per, lanes)
        for j in range(rows // per)
    ]
    return jnp.concatenate(parts, axis=1)


def project_kernel(a_ref, b_ref, c_ref, d_ref, w_ref, mine_ref, theirs_ref):
    weight = half_weight(w_ref)
    tok = a_ref.shape[0]
    for n, x_ref in enumerate((a_ref, b_ref, c_ref, d_ref)):
        out_ref = (mine_ref, theirs_ref)[n // 2]
        out_ref[pl.ds(n % 2 * tok, tok), :] = dot(x_ref[...], weight).astype(jnp.bfloat16)


def send_kernel(experts, mine_ref, swapped_ref, place_ref, out_ref, scr):
    first_plane = lax.axis_index("dp") % 2 == 0
    mine, swapped = mine_ref[...], swapped_ref[...]
    latent = jnp.where(first_plane, mine, swapped)
    grad = jnp.where(first_plane, swapped, mine)
    both = jnp.concatenate([latent, grad], axis=1)
    tok = both.shape[0] // 2
    chunks = both.shape[1] // LANES
    block = 2 * SLOTS * chunks
    for half in range(2):
        for s in range(SLOTS):
            rows = dot(place_ref[half * SLOTS + s], both[half * tok : (half + 1) * tok])
            for j in range(chunks):
                first = ((half * SLOTS + s) * chunks + j) * PITCH
                scr[pl.ds(first, experts), :] = rows[:, j * LANES : (j + 1) * LANES]
    for e in range(experts):
        out_ref[pl.ds(e * block, block), :] = scr[pl.ds(e, block, stride=PITCH), :].astype(jnp.bfloat16)


def expert_kernel(chips, in_ref, up_ref, down_ref, out_ref, scr, lat, grad, made, done, sems):
    width = lat.shape[1]
    chunks = width // LANES
    block = 2 * SLOTS * chunks
    scr[...] = in_ref[...].astype(jnp.float32)
    for core in range(2):
        for s in range(SLOTS):
            for j in range(chunks):
                sender, part = divmod(j, chunks // 2)
                slot = s if sender == core else SLOTS + s
                at = (pl.ds((core * SLOTS + s) * chips, chips), pl.ds(j * LANES, LANES))
                first = sender * block + slot * chunks + part
                lat[at] = scr[pl.ds(first, chips, stride=2 * block), :].astype(jnp.bfloat16)
                first += chunks // 2
                grad[at] = scr[pl.ds(first, chips, stride=2 * block), :].astype(jnp.bfloat16)
    tiles = 2
    per = lat.shape[0] // tiles
    slots_per = per // chips
    for m in range(tiles):
        at = pl.ds(m * per, per)
        act = jnp.maximum(dot(lat[at, :], up_ref[...]), 0.0)
        squared = jnp.square(act).astype(jnp.bfloat16)
        out = dot(squared, down_ref[...])
        grad_act = contract_last(grad[at, :], down_ref[...])
        grad_pre = (2.0 * act * grad_act).astype(jnp.bfloat16)
        back = contract_last(grad_pre, up_ref[...])
        for q in range(slots_per):
            core, s = divmod(m * slots_per + q, SLOTS)
            for j in range(chunks):
                part = (slice(q * chips, (q + 1) * chips), slice(j * LANES, (j + 1) * LANES))
                first = (s * chunks + j) * PITCH + core * chips
                made[pl.ds(first, chips), :] = out[part]
                made[pl.ds(first + block // 2 * PITCH, chips), :] = back[part]
    parts = sems.shape[0]
    copies = []
    for n in range(parts):
        for chip in range(n * chips // parts, (n + 1) * chips // parts):
            for core in range(2):
                rows = made[pl.ds(core * chips + chip, block, stride=PITCH), :]
                done[pl.ds((2 * chip + core) * block, block), :] = rows.astype(jnp.bfloat16)
        at = pl.ds(n * (2 * chips * block // parts), 2 * chips * block // parts)
        copies.append(pltpu.make_async_copy(done.at[at], out_ref.at[at], sems.at[n]))
        copies[-1].start()
    for copy in copies:
        copy.wait()


def finish_kernel(
    experts, high_ref, low_ref, same_ref, next_ref, plane_ref, far_ref, in_ref, layer_ref, grad_ref,
    scr, rows, landed, sems,
):
    chunks = rows.shape[1] // (2 * LANES)
    block = 2 * SLOTS * chunks
    per = in_ref.shape[0] // sems.shape[0]
    pieces = [pl.ds(n * per, per) for n in range(sems.shape[0])]
    copies = [
        pltpu.make_async_copy(in_ref.at[at], landed.at[at], sems.at[n]) for n, at in enumerate(pieces)
    ]
    for copy in copies:
        copy.start()
    for copy, at in zip(copies, pieces):
        copy.wait()
        scr[at, :] = landed[at, :].astype(jnp.float32)
    for s in range(SLOTS):
        for kind in range(2):
            for j in range(chunks):
                first = (kind * SLOTS + s) * chunks + j
                at = (pl.ds(s * experts, experts), pl.ds((kind * chunks + j) * LANES, LANES))
                rows[at] = scr[pl.ds(first, experts, stride=block), :].astype(jnp.bfloat16)
    total = dot(high_ref[...], rows[...]) + dot(low_ref[...], rows[...])
    total = total.astype(jnp.bfloat16)
    first_plane, first_core = lax.axis_index("dp") % 2 == 0, lax.axis_index("ep") % 2 == 0
    half = chunks * LANES // 2

    def swapped(yes, x):
        return jnp.concatenate(
            [jnp.where(yes, x[:, :half], x[:, half:]), jnp.where(yes, x[:, half:], x[:, :half])], axis=1
        )

    combined = swapped(first_core, total[:, : 2 * half])
    grad_sum = swapped(first_core, total[:, 2 * half :])
    mine = jnp.where(first_plane, grad_sum, combined)
    theirs = jnp.where(first_plane, combined, grad_sum)

    def project(x, this, that):
        return contract_last(x, jnp.concatenate([half_weight(this), half_weight(that)], axis=1))

    mine = project(mine, same_ref, next_ref)
    theirs = project(theirs, plane_ref, far_ref)
    layer_ref[...] = jnp.where(first_plane, theirs, mine).astype(jnp.bfloat16)
    grad_ref[...] = jnp.where(first_plane, mine, theirs).astype(jnp.bfloat16)


def on_device(tokens, expert_ids, gate_values, latent_down, latent_up, expert_up, expert_down, grad_out):
    ep, dp = lax.axis_size("ep"), lax.axis_size("dp")
    tok, wide = tokens.shape
    shard, width = latent_down.shape
    hidden = expert_up.shape[2]
    chunks = width // LANES
    block = 2 * SLOTS * chunks
    bf16, f32 = jnp.bfloat16, jnp.float32

    def beside(x):
        return lax.ppermute(x, "ep", [(i, i ^ 1) for i in range(ep)])

    def next_plane(x):
        return lax.ppermute(x, "dp", [(i, i ^ 1) for i in range(dp)])

    def exchange(x):
        return lax.all_to_all(x, "ep", split_axis=0, concat_axis=0, tiled=True)

    cast = vmem_call(
        cast_kernel,
        jax.ShapeDtypeStruct((ep // 2, chunks * shard, LANES), bf16),
        [
            pltpu.VMEM((shard, width), bf16),
            pltpu.VMEM((ep // 8, chunks * shard, LANES), bf16),
            pltpu.SemaphoreType.DMA,
            pltpu.SemaphoreType.DMA((4,)),
        ],
        61,
        0,
        MIB,
        arrays=0,
        far=2,
        far_out=True,
    )(latent_down, latent_up.T)
    same = exchange(cast.reshape(ep, chunks // 2 * shard, LANES))

    first_plane = lax.axis_index("dp") % 2 == 0
    own = jnp.where(first_plane, tokens, grad_out)
    theirs = next_plane(jnp.where(first_plane, grad_out, tokens))
    own_ids = expert_ids.T

    place, high, low = vmem_call(
        functools.partial(route_kernel, ep),
        (
            jax.ShapeDtypeStruct((2 * SLOTS, ep, tok), bf16),
            jax.ShapeDtypeStruct((tok, SLOTS * ep), bf16),
            jax.ShapeDtypeStruct((tok, SLOTS * ep), bf16),
        ),
        [],
        8,
        4 * tok * tok * ep,
        MIB,
        arrays=3,
    )(own_ids, beside(own_ids), gate_values.T)

    own_after, place, high, low = lax.optimization_barrier((own, place, high, low))
    projected = jax.ShapeDtypeStruct((2 * tok, width // 2), bf16)
    mine, away = vmem_call(
        project_kernel,
        (projected, projected),
        [],
        12,
        4 * tok * wide * width,
        4 * MIB,
        arrays=5,
    )(own_after, beside(own), theirs, beside(theirs), same)

    outbound = vmem_call(
        functools.partial(send_kernel, ep),
        jax.ShapeDtypeStruct((ep * block, LANES), bf16),
        [pltpu.VMEM((block * PITCH, LANES), f32)],
        12,
        4 * SLOTS * tok * ep * width,
        3 * MIB,
        arrays=3,
    )(mine, next_plane(away), place)

    arrived = exchange(outbound.reshape(ep, block, LANES))
    other = next_plane(same)

    rows = ep // 2 * 2 * SLOTS
    done = vmem_call(
        functools.partial(expert_kernel, ep // 2),
        jax.ShapeDtypeStruct((ep * block, LANES), bf16),
        [
            pltpu.VMEM((ep * block, LANES), f32),
            pltpu.VMEM((rows, width), bf16),
            pltpu.VMEM((rows, width), bf16),
            pltpu.VMEM((block * PITCH, LANES), f32),
            pltpu.VMEM((ep * block, LANES), bf16),
            pltpu.SemaphoreType.DMA((4,)),
        ],
        36,
        8 * rows * width * hidden,
        8 * MIB,
        arrays=3,
        far_out=True,
    )(arrived.reshape(ep * block, LANES), expert_up[0], expert_down[0])

    returned = exchange(done.reshape(ep, block, LANES))
    result = jax.ShapeDtypeStruct((tok, wide), bf16)
    return vmem_call(
        functools.partial(finish_kernel, ep),
        (result, result),
        [
            pltpu.VMEM((ep * block, LANES), f32),
            pltpu.VMEM((SLOTS * ep, 2 * width), bf16),
            pltpu.VMEM((ep * block, LANES), bf16),
            pltpu.SemaphoreType.DMA((4,)),
        ],
        51,
        4 * tok * wide * width,
        7 * MIB,
        arrays=6,
        far=1,
    )(high, low, same, beside(same), other, beside(other), returned.reshape(ep * block, LANES))


def solution(mesh):
    rows = P(("dp", "ep"), None)
    experts = P("ep", None, None)
    return jax.shard_map(
        on_device,
        mesh=mesh,
        in_specs=(rows, rows, rows, P("ep", None), P(None, "ep"), experts, experts, rows),
        out_specs=(rows, rows),
        check_vma=False,
    )
```
